32 devices in a mesh: rows: 8 (over z, y), pair: 4 (over x, core).
Axes of the slice: x: 2, y: 2, z: 4, core: 2. Of those that a mesh axis runs over, the one named last changes fastest.
Arguments:
- a_tiles: bfloat16 [2048, 8, 4096], P(('rows', 'pair')), may hold values from -2.09375 to 2.09375
- p_tiles: bfloat16 [2048, 4096], P(('rows', 'pair')), may hold values from -0.75 to 0.75
- a_cols: int32 [2048, 8], P(('rows', 'pair')), may hold values from 0 to 2047, as said below
- tile_group: int32 [2048, 8], P(('rows', 'pair')), may hold values from 0 to 1
- coarse_slots: int32 [2048, 2], P(('rows', 'pair')), may hold values from 0 to 15
- aggregate: int32 [2048], P(('rows', 'pair')), may hold values from 0 to 127, as said below
Outputs:
- coarse_tiles: float32 [128, 16, 4096], P(('rows', 'pair'))
The draws below stay inside these ranges and needn't reach their ends.
Inputs may be any that keep to these rules, and one draw needn't show every extreme that they name: `a_cols`: each operator tile's column block lies within 2 block rows of its own block row. `aggregate`: coarse block rows come in groups of 16 consecutive ones, group g held by index g of rows; the fine block rows of one device name at most 16 rows of one group, and one group, drawn from the seed, gets exactly 16 from every device.
All inputs are finite; a program needn't handle non-finite values.
Results may differ from the reference program's by a relative error of at most 0.0041.
Values may be sent and summed in bfloat16 or wider, within the bound.
A program may use at most 128 MiB of HBM per device.

```python
import jax
import jax.numpy as jnp
from jax import lax

BLK = 64
KA = 8
KS = 2
KC = 16
HB = 2
FB = 64
CB = 4
NF = 2048
NC = 128
N_ROWS = 8
N_PAIR = 4


def draw_a_cols(key, part):
    row_ids = jnp.arange(NF, dtype=jnp.int32)
    offset = jax.random.randint(key, (NF, KA), -HB, HB + 1, dtype=jnp.int32)
    return jnp.clip(row_ids[:, None] + offset, 0, NF - 1).astype(jnp.int32)


def draw_aggregate(key, part):
    capacity = 2 * FB // N_ROWS
    group_size = CB * N_PAIR
    busy_group = jax.random.randint(jax.random.fold_in(key, 1), (), 0, N_ROWS, dtype=jnp.int32)

    def one_device(device):
        device_key = jax.random.fold_in(key, device + 7)
        slot_ids = jax.random.permutation(jax.random.fold_in(device_key, 1), (N_ROWS - 1) * capacity)[:FB - capacity]
        others = (slot_ids // capacity).astype(jnp.int32)
        others = others + (others >= busy_group).astype(jnp.int32)
        groups = jnp.concatenate([jnp.full((capacity,), busy_group, jnp.int32), others])
        order_rows = jax.random.permutation(jax.random.fold_in(device_key, 2), FB)
        groups = groups[order_rows]
        local_rows = jax.random.randint(jax.random.fold_in(device_key, 3), (FB,), 0, group_size, dtype=jnp.int32)
        return groups * group_size + local_rows
    return jax.vmap(one_device)(jnp.arange(N_ROWS * N_PAIR, dtype=jnp.int32)).reshape(-1).astype(jnp.int32)


def with_ends(drawn, key, low, high):
    extent = drawn.shape
    place = [jax.random.randint(jax.random.fold_in(key, axis), (), 0, extent[axis]) for axis in range(len(extent))]
    drawn = drawn.at[tuple(place)].set(low)
    longest = extent.index(max(extent))
    place[longest] = (place[longest] + 1) % extent[longest]
    return drawn.at[tuple(place)].set(high)


def shard_levels(own_key, dims, cuts, low, top_value):
    level = 1.0
    for dim, shards_of in cuts:
        heights = jax.random.uniform(jax.random.fold_in(jax.random.fold_in(own_key, 6), dim), (shards_of,), jnp.float32, low / len(cuts), top_value / len(cuts))
        level = level * jnp.repeat(jnp.exp(heights), dims[dim] // shards_of).reshape((-1,) + (1,) * (len(dims) - 1 - dim))
    return level


def gaussian(rng, extent, deviation, reach, pieces=(), kind=jnp.bfloat16):
    gain = shard_levels(rng, extent, pieces, -0.22, 0.18) if pieces else 1.0
    drawn = jax.random.normal(rng, extent, jnp.float32) * deviation * gain
    return jnp.minimum(jnp.maximum(drawn, -reach), reach).astype(kind)


def setup_inputs(seed: int = 0) -> dict:
    streams_of = jax.random.split(jax.random.key(seed), 7)
    a_tiles = gaussian(streams_of[0], (NF, KA, BLK * BLK), 0.35, 2.09375, ((0, 32),))
    p_tiles = gaussian(streams_of[1], (NF, BLK * BLK), BLK ** -0.5, 0.75, ((0, 32),))
    a_cols = draw_a_cols(jax.random.fold_in(streams_of[6], 71), 0)
    tile_group = with_ends(jax.random.randint(streams_of[3], (NF, KA), 0, KS), jax.random.fold_in(streams_of[3], 1), 0, KS - 1).astype(jnp.int32)
    coarse_slots = with_ends(jax.random.randint(streams_of[4], (NF, KS), 0, KC), jax.random.fold_in(streams_of[4], 1), 0, KC - 1).astype(jnp.int32)
    aggregate = draw_aggregate(jax.random.fold_in(streams_of[6], 71), 0)
    return dict(a_tiles=a_tiles, p_tiles=p_tiles, a_cols=a_cols, tile_group=tile_group, coarse_slots=coarse_slots, aggregate=aggregate)


def reshape_blocks(values):
    return values.reshape((NF // FB, FB) + values.shape[1:])


def reference(a_tiles, p_tiles, a_cols, tile_group, coarse_slots, aggregate):
    def advance(carry, inputs):
        a_block, col_block, pick_block, slot_block, agg_block, own_block = inputs
        near_tiles = p_tiles[col_block].astype(jnp.float32).reshape(FB, KA, BLK, BLK)
        a_float = a_block.astype(jnp.float32).reshape(FB, KA, BLK, BLK)
        products = jnp.einsum("tkab,tkbc->tkac", a_float, near_tiles).astype(jnp.bfloat16)
        products = products.reshape(FB, KA, BLK * BLK).astype(jnp.float32)
        selector = (pick_block[:, :, None] == jnp.arange(KS, dtype=jnp.int32)[None, None, :]).astype(jnp.float32)
        slot_sums = jnp.einsum("tks,tkf->tsf", selector, products).astype(jnp.bfloat16)
        own_float = own_block.astype(jnp.float32).reshape(FB, BLK, BLK)
        terms = jnp.einsum("tji,tsjc->tsic", own_float, slot_sums.astype(jnp.float32).reshape(FB, KS, BLK, BLK))
        terms = terms.reshape(FB * KS, BLK * BLK)
        targets = (agg_block[:, None] * KC + slot_block).reshape(-1).astype(jnp.int32)
        return carry.at[targets].add(terms), None

    start = jnp.zeros((NC * KC, BLK * BLK), jnp.float32)
    result, _ = lax.scan(advance, start, (reshape_blocks(a_tiles), reshape_blocks(a_cols), reshape_blocks(tile_group), reshape_blocks(coarse_slots), reshape_blocks(aggregate), reshape_blocks(p_tiles)))
    return result.reshape(NC, KC, BLK * BLK)
```

```python
import functools

import jax
import jax.numpy as jnp
from jax import lax
from jax.experimental import pallas as pl
from jax.experimental.pallas import tpu as pltpu
from jax.sharding import PartitionSpec as P

BLK = 64
KA = 8
KS = 2
KC = 16
HB = 2
RATIO = 16
LANES = 128
NEAR = 2 * HB + 1
CHUNK = 8
BOTH = ("rows", "pair")


def extended(array, width):
    devices, length = lax.axis_size(BOTH), array.shape[0]
    up = [(i, i + 1) for i in range(devices - 1)]
    down = [(j, i) for i, j in up]
    before = lax.ppermute(array[length - width :], BOTH, up)
    after = lax.ppermute(array[:width], BOTH, down)
    return jnp.concatenate([before, array, after], axis=0)


def iota(shape, dim):
    return lax.broadcasted_iota(jnp.int32, shape, dim)


def terms_kernel(a_ref, p_ref, code_ref, group_ref, out_ref, diag, stage):
    step = pl.program_id(0)
    count = p_ref.shape[0]
    q = BLK // 2

    @pl.when(step == 0)
    def _():
        r, k = iota((LANES, LANES), 0), iota((LANES, LANES), 1)
        want = jnp.where(
            (r // BLK == k // BLK) & (r % BLK == 2 * (k % q) + (k // q) % 2), 1.0, 0.0
        ).astype(jnp.bfloat16)
        low = iota((q, LANES), 1) < BLK

        def one(t, _):
            flat = p_ref[t].astype(jnp.float32)
            turned = pltpu.roll(flat, BLK, 1)
            zero = jnp.zeros_like(flat)
            parts = jnp.concatenate(
                [
                    jnp.where(low, flat, zero),
                    jnp.where(low, turned, zero),
                    jnp.where(low, zero, turned),
                    jnp.where(low, zero, flat),
                ],
                axis=0,
            ).astype(jnp.bfloat16)
            diag[pl.ds(pl.multiple_of(t * LANES, LANES), LANES), :] = jnp.dot(
                want, parts, preferred_element_type=jnp.float32
            ).astype(jnp.bfloat16)
            return 0

        lax.fori_loop(0, count, one, 0, unroll=4)

    eye = jnp.where(iota((LANES, LANES), 0) == iota((LANES, LANES), 1), 1.0, 0.0).astype(
        jnp.bfloat16
    )
    spread = jnp.where(
        iota((q, q * KA), 0) == iota((q, q * KA), 1) // KA, 1.0, 0.0
    ).astype(jnp.bfloat16)
    low = iota((q, LANES), 1) < BLK

    for i in range(CHUNK):
        row = step * CHUNK + i
        code = code_ref[i]
        masks = [code == j for j in range(NEAR)]
        columns = []
        for j in range(NEAR):
            pieces = []
            for c in range(q):
                piece = a_ref[i, :, c * LANES : (c + 1) * LANES].astype(jnp.float32)
                pieces.append(jnp.where(masks[j], piece, 0.0))
            columns.append(jnp.concatenate(pieces, axis=0).astype(jnp.bfloat16))
        left = jnp.concatenate(columns, axis=1)
        near = diag[pl.ds(pl.multiple_of(row * LANES, LANES), NEAR * LANES), :]
        products = jnp.dot(left, near, preferred_element_type=jnp.float32).astype(jnp.bfloat16)
        own = p_ref[row + HB]
        turned = lax.dot_general(
            eye, own, (((1,), (1,)), ((), ())), preferred_element_type=jnp.float32
        ).astype(jnp.bfloat16)
        wide = jnp.dot(turned, spread, preferred_element_type=jnp.float32)
        group = group_ref[i]
        rows = jnp.concatenate(
            [jnp.where(group == s, wide, 0.0) for s in range(KS)], axis=0
        ).astype(jnp.bfloat16)
        full = jnp.dot(rows, products, preferred_element_type=jnp.float32)
        for s in range(KS):
            part = full[s * LANES : (s + 1) * LANES]
            term = jnp.where(low, part[:q], part[3 * q :]) + pltpu.roll(
                jnp.where(low, part[q : 2 * q], part[2 * q : 3 * q]), BLK, 1
            )
            stage[pl.ds(s * CHUNK + i, q, stride=KS * CHUNK), :] = term
    out_ref[...] = stage[...].astype(jnp.bfloat16).reshape(out_ref.shape)


def local_terms(a_tiles, p_tiles, a_cols, tile_group):
    fine_rows = a_tiles.shape[0]
    device = lax.axis_index(BOTH)
    q = BLK // 2
    near_p = extended(p_tiles, HB).reshape(fine_rows + 2 * HB, q, LANES)
    own = device * fine_rows + jnp.arange(fine_rows, dtype=jnp.int32)
    offset = a_cols - own[:, None] + HB
    code = jnp.broadcast_to(offset[:, :, None], (fine_rows, KA, LANES))
    group = jnp.tile(tile_group, (1, q)).reshape(fine_rows, 1, q * KA)
    steps = fine_rows // CHUNK
    return pl.pallas_call(
        terms_kernel,
        grid=(steps,),
        in_specs=[
            pl.BlockSpec((CHUNK, KA, BLK * BLK), lambda g: (g, 0, 0)),
            pl.BlockSpec((fine_rows + 2 * HB, q, LANES), lambda g: (0, 0, 0)),
            pl.BlockSpec((CHUNK, KA, LANES), lambda g: (g, 0, 0)),
            pl.BlockSpec((CHUNK, 1, q * KA), lambda g: (g, 0, 0)),
        ],
        out_specs=pl.BlockSpec((q, KS * CHUNK, LANES), lambda g: (0, g, 0)),
        out_shape=jax.ShapeDtypeStruct((q, fine_rows * KS, LANES), jnp.bfloat16),
        scratch_shapes=[
            pltpu.VMEM(((fine_rows + 2 * HB) * LANES, LANES), jnp.bfloat16),
            pltpu.VMEM((q * KS * CHUNK, LANES), jnp.float32),
        ],
        compiler_params=pltpu.CompilerParams(vmem_limit_bytes=40 * 1024 * 1024),
    )(a_tiles, near_p, code, group)


def in_term_order(values):
    rows = values.shape[0]
    return values.reshape(rows // CHUNK, CHUNK, KS).transpose(0, 2, 1).reshape(rows * KS)


def sum_kernel(tile_rows, target_ref, term_ref, out_ref):
    first = pl.program_id(0) * tile_rows
    tiles = first + iota((tile_rows, target_ref.shape[1]), 0)
    hot = jnp.where(tiles == target_ref[...], 1.0, 0.0).astype(jnp.bfloat16)
    out_ref[...] = jnp.dot(hot, term_ref[...], preferred_element_type=jnp.float32).astype(
        jnp.bfloat16
    )


def sum_terms(targets, terms, tiles):
    tile_rows = 256
    count = terms.shape[0]
    return pl.pallas_call(
        functools.partial(sum_kernel, tile_rows),
        grid=(tiles // tile_rows,),
        in_specs=[
            pl.BlockSpec((1, count), lambda g: (0, 0)),
            pl.BlockSpec((count, LANES), lambda g: (0, 0)),
        ],
        out_specs=pl.BlockSpec((tile_rows, LANES), lambda g: (g, 0)),
        out_shape=jax.ShapeDtypeStruct((tiles, LANES), jnp.bfloat16),
        compiler_params=pltpu.CompilerParams(vmem_limit_bytes=40 * 1024 * 1024),
    )(targets, terms)


def join_kernel(in_ref, out_ref):
    devices, tiles = in_ref.shape[:2]
    low = iota((tiles, LANES), 1) < BLK
    half = devices * BLK
    for m in range(devices // 2):
        one, two = in_ref[2 * m].astype(jnp.float32), in_ref[2 * m + 1].astype(jnp.float32)
        at = m * LANES
        out_ref[:, at : at + LANES] = jnp.where(low, one, pltpu.roll(two, BLK, 1))
        out_ref[:, half + at : half + at + LANES] = jnp.where(low, pltpu.roll(one, BLK, 1), two)


def join(parts):
    devices, tiles, _ = parts.shape
    return pl.pallas_call(
        join_kernel,
        out_shape=jax.ShapeDtypeStruct((tiles, devices * LANES), jnp.float32),
    )(parts)


def routed(terms, coarse_slots, aggregate):
    fine_rows = aggregate.shape[0]
    q = BLK // 2
    width = BLK * BLK
    rows_count, pair_count = lax.axis_size("rows"), lax.axis_size("pair")
    flat = terms.reshape(q, fine_rows // CHUNK, KS, CHUNK, 2, BLK)
    flat = flat.transpose(1, 3, 2, 4, 0, 5).reshape(fine_rows, KS, width)
    group_size = fine_rows // RATIO * pair_count
    capacity = 2 * fine_rows // rows_count
    dest_group = aggregate // group_size
    local_rows = aggregate - dest_group * group_size
    targets = local_rows[:, None] * KC + coarse_slots
    order = jnp.arange(fine_rows)
    same = (dest_group[:, None] == dest_group[None, :]) & (order[None, :] < order[:, None])
    position = dest_group * capacity + jnp.sum(same.astype(jnp.int32), axis=1)

    def exchange(values):
        buffer = jnp.zeros((rows_count * capacity,) + values.shape[1:], values.dtype)
        buffer = buffer.at[position].set(values)
        return lax.all_to_all(buffer, "rows", split_axis=0, concat_axis=0, tiled=True)

    got = exchange(flat).reshape(-1, width).astype(jnp.float32)
    panel = jax.ops.segment_sum(
        got, exchange(targets).reshape(-1), num_segments=group_size * KC
    )
    panel = panel.reshape(group_size, KC, width)
    return lax.psum_scatter(panel, "pair", scatter_dimension=0, tiled=True)


def body(a_tiles, p_tiles, a_cols, tile_group, coarse_slots, aggregate):
    fine_rows, width = p_tiles.shape
    devices = lax.axis_size(BOTH)
    terms = local_terms(a_tiles, p_tiles, a_cols, tile_group)
    if devices * LANES != width:
        return routed(terms, coarse_slots, aggregate)
    tiles = fine_rows // RATIO * KC
    targets = in_term_order(aggregate[:, None] * KC + coarse_slots)
    targets = lax.all_gather(targets, BOTH, axis=0, tiled=True).reshape(1, -1)
    got = lax.all_to_all(terms, BOTH, split_axis=0, concat_axis=0, tiled=True)
    sums = sum_terms(targets, got.reshape(-1, LANES), devices * tiles)
    parts = lax.all_to_all(
        sums.reshape(devices, tiles, LANES), BOTH, split_axis=0, concat_axis=0, tiled=True
    )
    return join(parts).reshape(fine_rows // RATIO, KC, width)


def solution(mesh):
    return jax.shard_map(
        body,
        mesh=mesh,
        in_specs=(
            P(BOTH, None, None),
            P(BOTH, None),
            P(BOTH, None),
            P(BOTH, None),
            P(BOTH, None),
            P(BOTH),
        ),
        out_specs=P(BOTH, None, None),
        check_vma=False,
    )
```

```python
import functools

import jax
import jax.numpy as jnp
from jax import lax
from jax.experimental import pallas as pl
from jax.experimental.pallas import tpu as pltpu
from jax.sharding import PartitionSpec as P

BLK = 64
KA = 8
KS = 2
KC = 16
HB = 2
RATIO = 16
LANES = 128
NEAR = 2 * HB + 1
CHUNK = 8
BOTH = ("rows", "pair")


def extended(array, width):
    devices, length = lax.axis_size(BOTH), array.shape[0]
    up = [(i, i + 1) for i in range(devices - 1)]
    down = [(j, i) for i, j in up]
    before = lax.ppermute(array[length - width :], BOTH, up)
    after = lax.ppermute(array[:width], BOTH, down)
    return jnp.concatenate([before, array, after], axis=0)


def iota(shape, dim):
    return lax.broadcasted_iota(jnp.int32, shape, dim)


def terms_kernel(a_ref, p_ref, code_ref, group_ref, out_ref, diag, stage):
    step = pl.program_id(0)
    count = p_ref.shape[0]
    q = BLK // 2

    @pl.when(step == 0)
    def _():
        r, k = iota((LANES, LANES), 0), iota((LANES, LANES), 1)
        want = jnp.where(
            (r // BLK == k // BLK) & (r % BLK == 2 * (k % q) + (k // q) % 2), 1.0, 0.0
        ).astype(jnp.bfloat16)
        low = iota((q, LANES), 1) < BLK

        def one(t, _):
            flat = p_ref[t].astype(jnp.float32)
            turned = pltpu.roll(flat, BLK, 1)
            zero = jnp.zeros_like(flat)
            parts = jnp.concatenate(
                [
                    jnp.where(low, flat, zero),
                    jnp.where(low, turned, zero),
                    jnp.where(low, zero, turned),
                    jnp.where(low, zero, flat),
                ],
                axis=0,
            ).astype(jnp.bfloat16)
            diag[pl.ds(pl.multiple_of(t * LANES, LANES), LANES), :] = jnp.dot(
                want, parts, preferred_element_type=jnp.float32
            ).astype(jnp.bfloat16)
            return 0

        lax.fori_loop(0, count, one, 0, unroll=4)

    eye = jnp.where(iota((LANES, LANES), 0) == iota((LANES, LANES), 1), 1.0, 0.0).astype(
        jnp.bfloat16
    )
    spread = jnp.where(
        iota((q, q * KA), 0) == iota((q, q * KA), 1) // KA, 1.0, 0.0
    ).astype(jnp.bfloat16)
    low = iota((q, LANES), 1) < BLK

    for i in range(CHUNK):
        row = step * CHUNK + i
        code = code_ref[i]
        masks = [code == j for j in range(NEAR)]
        columns = []
        for j in range(NEAR):
            pieces = []
            for c in range(q):
                piece = a_ref[i, :, c * LANES : (c + 1) * LANES].astype(jnp.float32)
                pieces.append(jnp.where(masks[j], piece, 0.0))
            columns.append(jnp.concatenate(pieces, axis=0).astype(jnp.bfloat16))
        left = jnp.concatenate(columns, axis=1)
        near = diag[pl.ds(pl.multiple_of(row * LANES, LANES), NEAR * LANES), :]
        products = jnp.dot(left, near, preferred_element_type=jnp.float32).astype(jnp.bfloat16)
        own = p_ref[row + HB]
        turned = lax.dot_general(
            eye, own, (((1,), (1,)), ((), ())), preferred_element_type=jnp.float32
        ).astype(jnp.bfloat16)
        wide = jnp.dot(turned, spread, preferred_element_type=jnp.float32)
        group = group_ref[i]
        rows = jnp.concatenate(
            [jnp.where(group == s, wide, 0.0) for s in range(KS)], axis=0
        ).astype(jnp.bfloat16)
        full = jnp.dot(rows, products, preferred_element_type=jnp.float32)
        for s in range(KS):
            part = full[s * LANES : (s + 1) * LANES]
            term = jnp.where(low, part[:q], part[3 * q :]) + pltpu.roll(
                jnp.where(low, part[q : 2 * q], part[2 * q : 3 * q]), BLK, 1
            )
            stage[pl.ds(s * CHUNK + i, q, stride=KS * CHUNK), :] = term
    out_ref[...] = stage[...].astype(jnp.bfloat16).reshape(out_ref.shape)


def local_terms(a_tiles, p_tiles, a_cols, tile_group):
    fine_rows = a_tiles.shape[0]
    device = lax.axis_index(BOTH)
    q = BLK // 2
    near_p = extended(p_tiles, HB).reshape(fine_rows + 2 * HB, q, LANES)
    own = device * fine_rows + jnp.arange(fine_rows, dtype=jnp.int32)
    offset = a_cols - own[:, None] + HB
    code = jnp.broadcast_to(offset[:, :, None], (fine_rows, KA, LANES))
    group = jnp.tile(tile_group, (1, q)).reshape(fine_rows, 1, q * KA)
    steps = fine_rows // CHUNK
    return pl.pallas_call(
        terms_kernel,
        grid=(steps,),
        in_specs=[
            pl.BlockSpec((CHUNK, KA, BLK * BLK), lambda g: (g, 0, 0)),
            pl.BlockSpec((fine_rows + 2 * HB, q, LANES), lambda g: (0, 0, 0)),
            pl.BlockSpec((CHUNK, KA, LANES), lambda g: (g, 0, 0)),
            pl.BlockSpec((CHUNK, 1, q * KA), lambda g: (g, 0, 0)),
        ],
        out_specs=pl.BlockSpec((q, KS * CHUNK, LANES), lambda g: (0, g, 0)),
        out_shape=jax.ShapeDtypeStruct((q, fine_rows * KS, LANES), jnp.bfloat16),
        scratch_shapes=[
            pltpu.VMEM(((fine_rows + 2 * HB) * LANES, LANES), jnp.bfloat16),
            pltpu.VMEM((q * KS * CHUNK, LANES), jnp.float32),
        ],
        compiler_params=pltpu.CompilerParams(vmem_limit_bytes=40 * 1024 * 1024),
    )(a_tiles, near_p, code, group)


def in_term_order(values):
    rows = values.shape[0]
    return values.reshape(rows // CHUNK, CHUNK, KS).transpose(0, 2, 1).reshape(rows * KS)


def exchange_kernel(rows_count, pair_count, term_ref, target_ref, out_ref, got, goals, sums, parts, sent, came, goal_sent, goal_came, sum_sent, sum_came):
    my_row, my_pair = lax.axis_index("rows"), lax.axis_index("pair")
    devices = rows_count * pair_count
    me = my_row * pair_count + my_pair
    tiles = parts.shape[1]
    block = pair_count * tiles

    def at(device):
        return (lax.div(device, pair_count), lax.rem(device, pair_count))

    def copy(src, dst, send_sem, recv_sem, device):
        return pltpu.make_async_remote_copy(
            src_ref=src,
            dst_ref=dst,
            send_sem=send_sem,
            recv_sem=recv_sem,
            device_id=at(device),
            device_id_type=pl.DeviceIdType.MESH,
        )

    def term_copy(device, slot):
        return copy(term_ref.at[device], got.at[slot], sent.at[device], came.at[slot], device)

    def goal_copy(device, slot):
        return copy(target_ref, goals.at[slot], goal_sent.at[device], goal_came.at[slot], device)

    def sum_copy(device, slot):
        rows = pl.ds(pl.multiple_of(device * tiles, tiles), tiles)
        return copy(sums.at[rows], parts.at[slot], sum_sent.at[device], sum_came.at[slot], device)

    barrier = pltpu.get_barrier_semaphore()
    offsets = sorted(range(1, devices), key=lambda o: abs(o - devices // 2))
    for o in offsets:
        pl.semaphore_signal(
            barrier, inc=1, device_id=at(lax.rem(me + o, devices)), device_id_type=pl.DeviceIdType.MESH
        )
    pl.semaphore_wait(barrier, devices - 1)

    for o in offsets:
        other = lax.rem(me + o, devices)
        term_copy(other, me).start()
        goal_copy(other, me).start()
    got[me] = term_ref[me]
    goals[me] = target_ref[...]
    for o in offsets[::-1]:
        other = lax.rem(me + o, devices)
        goal_copy(other, other).wait_recv()
        term_copy(other, other).wait_recv()

    goal = jnp.concatenate([goals[j] for j in range(devices)], axis=1)
    for k in sorted(range(rows_count), key=lambda o: abs(o - rows_count // 2)):
        row = lax.rem(my_row + k, rows_count)
        first = row * block
        hot = jnp.where(first + iota((block, goal.shape[1]), 0) == goal, 1.0, 0.0).astype(jnp.bfloat16)
        sums[pl.ds(pl.multiple_of(first, block), block), :] = jnp.dot(
            hot, got[...].reshape(-1, LANES), preferred_element_type=jnp.float32
        ).astype(jnp.bfloat16)
        for o in range(0 if k else 1, pair_count):
            other = row * pair_count + lax.rem(my_pair + o, pair_count)
            sum_copy(other, me).start()
    parts[me] = sums[pl.ds(pl.multiple_of(me * tiles, tiles), tiles), :]
    for o in offsets:
        other = lax.rem(me + o, devices)
        sum_copy(other, other).wait_recv()

    low = iota((tiles, LANES), 1) < BLK
    half = devices * BLK
    for m in range(devices // 2):
        one, two = parts[2 * m].astype(jnp.float32), parts[2 * m + 1].astype(jnp.float32)
        to = m * LANES
        out_ref[:, to : to + LANES] = jnp.where(low, one, pltpu.roll(two, BLK, 1))
        out_ref[:, half + to : half + to + LANES] = jnp.where(low, pltpu.roll(one, BLK, 1), two)
    for o in offsets:
        other = lax.rem(me + o, devices)
        term_copy(other, me).wait_send()
        goal_copy(other, me).wait_send()
        sum_copy(other, me).wait_send()


def exchanged(terms, targets, tiles):
    devices, count, _ = terms.shape
    rows_count, pair_count = lax.axis_size("rows"), lax.axis_size("pair")
    whole = pl.BlockSpec(memory_space=pltpu.VMEM)
    return pl.pallas_call(
        functools.partial(exchange_kernel, rows_count, pair_count),
        in_specs=[whole, whole],
        out_specs=whole,
        out_shape=jax.ShapeDtypeStruct((tiles, devices * LANES), jnp.float32),
        scratch_shapes=[
            pltpu.VMEM((devices, count, LANES), jnp.bfloat16),
            pltpu.VMEM((devices, 1, count), jnp.int32),
            pltpu.VMEM((devices * tiles, LANES), jnp.bfloat16),
            pltpu.VMEM((devices, tiles, LANES), jnp.bfloat16),
        ]
        + [pltpu.SemaphoreType.DMA((devices,))] * 6,
        compiler_params=pltpu.CompilerParams(
            collective_id=0, has_side_effects=True, vmem_limit_bytes=40 * 1024 * 1024
        ),
    )(terms, targets)


def routed(terms, coarse_slots, aggregate):
    fine_rows = aggregate.shape[0]
    q = BLK // 2
    width = BLK * BLK
    rows_count, pair_count = lax.axis_size("rows"), lax.axis_size("pair")
    flat = terms.reshape(q, fine_rows // CHUNK, KS, CHUNK, 2, BLK)
    flat = flat.transpose(1, 3, 2, 4, 0, 5).reshape(fine_rows, KS, width)
    group_size = fine_rows // RATIO * pair_count
    capacity = 2 * fine_rows // rows_count
    dest_group = aggregate // group_size
    local_rows = aggregate - dest_group * group_size
    targets = local_rows[:, None] * KC + coarse_slots
    order = jnp.arange(fine_rows)
    same = (dest_group[:, None] == dest_group[None, :]) & (order[None, :] < order[:, None])
    position = dest_group * capacity + jnp.sum(same.astype(jnp.int32), axis=1)

    def exchange(values):
        buffer = jnp.zeros((rows_count * capacity,) + values.shape[1:], values.dtype)
        buffer = buffer.at[position].set(values)
        return lax.all_to_all(buffer, "rows", split_axis=0, concat_axis=0, tiled=True)

    got = exchange(flat).reshape(-1, width).astype(jnp.float32)
    panel = jax.ops.segment_sum(
        got, exchange(targets).reshape(-1), num_segments=group_size * KC
    )
    panel = panel.reshape(group_size, KC, width)
    return lax.psum_scatter(panel, "pair", scatter_dimension=0, tiled=True)


def body(a_tiles, p_tiles, a_cols, tile_group, coarse_slots, aggregate):
    fine_rows, width = p_tiles.shape
    devices = lax.axis_size(BOTH)
    terms = local_terms(a_tiles, p_tiles, a_cols, tile_group)
    if devices * LANES != width:
        return routed(terms, coarse_slots, aggregate)
    tiles = fine_rows // RATIO * KC
    targets = in_term_order(aggregate[:, None] * KC + coarse_slots)
    result = exchanged(terms, targets.reshape(1, -1), tiles)
    return result.reshape(fine_rows // RATIO, KC, width)


def solution(mesh):
    return jax.shard_map(
        body,
        mesh=mesh,
        in_specs=(
            P(BOTH, None, None),
            P(BOTH, None),
            P(BOTH, None),
            P(BOTH, None),
            P(BOTH, None),
            P(BOTH),
        ),
        out_specs=P(BOTH, None, None),
        check_vma=False,
    )
```

```python
import functools

import jax
import jax.numpy as jnp
from jax import lax
from jax.experimental import pallas as pl
from jax.experimental.pallas import tpu as pltpu
from jax.sharding import PartitionSpec as P

BLK = 64
KA = 8
KS = 2
KC = 16
HB = 2
RATIO = 16
LANES = 128
NEAR = 2 * HB + 1
CHUNK = 8
BOTH = ("rows", "pair")


def extended(array, width):
    devices, length = lax.axis_size(BOTH), array.shape[0]
    up = [(i, i + 1) for i in range(devices - 1)]
    down = [(j, i) for i, j in up]
    before = lax.ppermute(array[length - width :], BOTH, up)
    after = lax.ppermute(array[:width], BOTH, down)
    return jnp.concatenate([before, array, after], axis=0)


def iota(shape, dim):
    return lax.broadcasted_iota(jnp.int32, shape, dim)


def put_diagonal(flat, want, low):
    flat = flat.astype(jnp.float32)
    turned = pltpu.roll(flat, BLK, 1)
    zero = jnp.zeros_like(flat)
    parts = jnp.concatenate(
        [
            jnp.where(low, flat, zero),
            jnp.where(low, turned, zero),
            jnp.where(low, zero, turned),
            jnp.where(low, zero, flat),
        ],
        axis=0,
    ).astype(jnp.bfloat16)
    return jnp.dot(want, parts, preferred_element_type=jnp.float32).astype(jnp.bfloat16)


def constants():
    q = BLK // 2
    r, k = iota((LANES, LANES), 0), iota((LANES, LANES), 1)
    want = jnp.where(
        (r // BLK == k // BLK) & (r % BLK == 2 * (k % q) + (k // q) % 2), 1.0, 0.0
    ).astype(jnp.bfloat16)
    eye = jnp.where(r == k, 1.0, 0.0).astype(jnp.bfloat16)
    spread = jnp.where(
        iota((q, q * KA), 0) == iota((q, q * KA), 1) // KA, 1.0, 0.0
    ).astype(jnp.bfloat16)
    low = iota((q, LANES), 1) < BLK
    return want, eye, spread, low


def row_terms(read, code, group, near, own, eye, spread, low):
    q = BLK // 2
    tiles = jnp.concatenate([read(c).astype(jnp.float32) for c in range(q)], axis=0)
    codes = jnp.broadcast_to(code[None], (q,) + code.shape).reshape(tiles.shape)
    left = jnp.concatenate(
        [jnp.where(codes == j, tiles, 0.0).astype(jnp.bfloat16) for j in range(NEAR)], axis=1
    )
    products = jnp.dot(left, near, preferred_element_type=jnp.float32).astype(jnp.bfloat16)
    turned = lax.dot_general(
        eye, own, (((1,), (1,)), ((), ())), preferred_element_type=jnp.float32
    ).astype(jnp.bfloat16)
    wide = jnp.dot(turned, spread, preferred_element_type=jnp.float32)
    rows = jnp.concatenate(
        [jnp.where(group == s, wide, 0.0) for s in range(KS)], axis=0
    ).astype(jnp.bfloat16)
    full = jnp.dot(rows, products, preferred_element_type=jnp.float32)
    terms = []
    for s in range(KS):
        part = full[s * LANES : (s + 1) * LANES]
        terms.append(
            jnp.where(low, part[:q], part[3 * q :])
            + pltpu.roll(jnp.where(low, part[q : 2 * q], part[2 * q : 3 * q]), BLK, 1)
        )
    return terms


def terms_kernel(a_ref, p_ref, code_ref, group_ref, out_ref, diag, stage):
    step = pl.program_id(0)
    q = BLK // 2
    want, eye, spread, low = constants()

    @pl.when(step == 0)
    def _():
        def one(t, _):
            diag[pl.ds(pl.multiple_of(t * LANES, LANES), LANES), :] = put_diagonal(p_ref[t], want, low)
            return 0

        lax.fori_loop(0, p_ref.shape[0], one, 0, unroll=4)

    for i in range(CHUNK):
        row = step * CHUNK + i
        terms = row_terms(
            lambda c: a_ref[i, :, c * LANES : (c + 1) * LANES],
            code_ref[i],
            group_ref[i],
            diag[pl.ds(pl.multiple_of(row * LANES, LANES), NEAR * LANES), :],
            p_ref[row + HB],
            eye,
            spread,
            low,
        )
        for s in range(KS):
            stage[pl.ds(s * CHUNK + i, q, stride=KS * CHUNK), :] = terms[s]
    out_ref[...] = stage[...].astype(jnp.bfloat16).reshape(out_ref.shape)


def row_codes(a_cols, tile_group):
    fine_rows = a_cols.shape[0]
    q = BLK // 2
    own = lax.axis_index(BOTH) * fine_rows + jnp.arange(fine_rows, dtype=jnp.int32)
    offset = a_cols - own[:, None] + HB
    code = jnp.broadcast_to(offset[:, :, None], (fine_rows, KA, LANES))
    group = jnp.tile(tile_group, (1, q)).reshape(fine_rows, 1, q * KA)
    return code, group


def local_terms(a_tiles, p_tiles, a_cols, tile_group):
    fine_rows = a_tiles.shape[0]
    q = BLK // 2
    near_p = extended(p_tiles, HB).reshape(fine_rows + 2 * HB, q, LANES)
    code, group = row_codes(a_cols, tile_group)
    steps = fine_rows // CHUNK
    return pl.pallas_call(
        terms_kernel,
        grid=(steps,),
        in_specs=[
            pl.BlockSpec((CHUNK, KA, BLK * BLK), lambda g: (g, 0, 0)),
            pl.BlockSpec((fine_rows + 2 * HB, q, LANES), lambda g: (0, 0, 0)),
            pl.BlockSpec((CHUNK, KA, LANES), lambda g: (g, 0, 0)),
            pl.BlockSpec((CHUNK, 1, q * KA), lambda g: (g, 0, 0)),
        ],
        out_specs=pl.BlockSpec((q, KS * CHUNK, LANES), lambda g: (0, g, 0)),
        out_shape=jax.ShapeDtypeStruct((q, fine_rows * KS, LANES), jnp.bfloat16),
        scratch_shapes=[
            pltpu.VMEM(((fine_rows + 2 * HB) * LANES, LANES), jnp.bfloat16),
            pltpu.VMEM((q * KS * CHUNK, LANES), jnp.float32),
        ],
        compiler_params=pltpu.CompilerParams(vmem_limit_bytes=40 * 1024 * 1024),
    )(a_tiles, near_p, code, group)


def in_term_order(values):
    rows = values.shape[0]
    return values.reshape(rows // CHUNK, CHUNK, KS).transpose(0, 2, 1).reshape(rows * KS)


def exchange_kernel(rows_count, pair_count, a_hbm, p_ref, code_ref, group_ref, target_ref, out_ref, a_ref, diag, stage, halo, term_ref, got, goals, sums, parts, a_came, halo_sent, halo_came, sent, came, goal_sent, goal_came, sum_sent, sum_came):
    my_row, my_pair = lax.axis_index("rows"), lax.axis_index("pair")
    devices = rows_count * pair_count
    me = my_row * pair_count + my_pair
    tiles = parts.shape[1]
    block = pair_count * tiles

    def at(device):
        return (lax.div(device, pair_count), lax.rem(device, pair_count))

    def copy(src, dst, send_sem, recv_sem, device):
        return pltpu.make_async_remote_copy(
            src_ref=src,
            dst_ref=dst,
            send_sem=send_sem,
            recv_sem=recv_sem,
            device_id=at(device),
            device_id_type=pl.DeviceIdType.MESH,
        )

    fine_rows = p_ref.shape[0]
    q = BLK // 2
    steps = 4
    span = fine_rows // steps
    terms_span = span * KS
    ahead, behind = lax.rem(me + 1, devices), lax.rem(me + devices - 1, devices)

    def a_copy(step):
        rows = pl.ds(pl.multiple_of(lax.rem(step + 1, steps) * span, span), span)
        return pltpu.make_async_copy(a_hbm.at[rows], a_ref.at[rows], a_came.at[step])

    def term_copy(device, slot):
        return copy(term_ref.at[device], got.at[slot], sent.at[device], came.at[slot], device)

    def term_part(device, slot, part):
        rows = pl.ds(pl.multiple_of(part * terms_span, terms_span), terms_span)
        return copy(term_ref.at[device, rows], got.at[slot, rows], sent.at[device], came.at[slot], device)

    halo_up = copy(p_ref.at[pl.ds(fine_rows - HB, HB)], halo.at[pl.ds(0, HB)], halo_sent.at[0], halo_came.at[0], ahead)
    halo_down = copy(p_ref.at[pl.ds(0, HB)], halo.at[pl.ds(HB, HB)], halo_sent.at[1], halo_came.at[1], behind)

    def goal_copy(device, slot):
        return copy(target_ref, goals.at[slot], goal_sent.at[device], goal_came.at[slot], device)

    def sum_copy(device, slot):
        rows = pl.ds(pl.multiple_of(device * tiles, tiles), tiles)
        return copy(sums.at[rows], parts.at[slot], sum_sent.at[device], sum_came.at[slot], device)

    barrier = pltpu.get_barrier_semaphore()
    offsets = sorted(range(1, devices), key=lambda o: abs(o - devices // 2))
    for o in offsets:
        pl.semaphore_signal(
            barrier, inc=1, device_id=at(lax.rem(me + o, devices)), device_id_type=pl.DeviceIdType.MESH
        )
    for step in range(steps):
        a_copy(step).start()
    want, eye, spread, low = constants()

    def own_diagonal(t, _):
        diag[pl.ds(pl.multiple_of((t + HB) * LANES, LANES), LANES), :] = put_diagonal(p_ref[t], want, low)
        return 0

    lax.fori_loop(0, fine_rows, own_diagonal, 0, unroll=4)
    pl.semaphore_wait(barrier, devices - 1)
    halo_up.start()
    halo_down.start()
    for o in offsets:
        other = lax.rem(me + o, devices)
        goal_copy(other, me).start()
    goals[me] = target_ref[...]

    def quarter(step, _):
        part = lax.rem(step + 1, steps)
        a_copy(step).wait()

        @pl.when(step == steps - 2)
        def _():
            halo_up.wait_recv()
            halo_down.wait_recv()
            for t in range(HB):
                diag[t * LANES : (t + 1) * LANES, :] = put_diagonal(halo[t], want, low)
                last = fine_rows + HB + t
                diag[last * LANES : (last + 1) * LANES, :] = put_diagonal(halo[HB + t], want, low)

        def chunk(c, _):
            at_chunk = part * (span // CHUNK) + c

            for i in range(CHUNK):
                row = at_chunk * CHUNK + i
                terms = row_terms(
                    lambda col: a_ref[row, :, col * LANES : (col + 1) * LANES],
                    code_ref[row],
                    group_ref[row],
                    diag[pl.ds(pl.multiple_of(row * LANES, LANES), NEAR * LANES), :],
                    p_ref[row],
                    eye,
                    spread,
                    low,
                )
                for s in range(KS):
                    stage[pl.ds(s * CHUNK + i, q, stride=KS * CHUNK), :] = terms[s]
            rows = pl.ds(pl.multiple_of(at_chunk * KS * CHUNK, KS * CHUNK), KS * CHUNK)
            term_ref[:, rows, :] = stage[...].astype(jnp.bfloat16).reshape(q, KS * CHUNK, LANES)
            return 0

        lax.fori_loop(0, span // CHUNK, chunk, 0)
        for o in offsets:
            term_part(lax.rem(me + o, devices), me, part).start()
        return 0

    lax.fori_loop(0, steps, quarter, 0)
    got[me] = term_ref[me]
    for o in offsets[::-1]:
        other = lax.rem(me + o, devices)
        goal_copy(other, other).wait_recv()
        term_copy(other, other).wait_recv()

    goal = jnp.concatenate([goals[j] for j in range(devices)], axis=1)
    for k in sorted(range(rows_count), key=lambda o: abs(o - rows_count // 2)):
        row = lax.rem(my_row + k, rows_count)
        first = row * block
        hot = jnp.where(first + iota((block, goal.shape[1]), 0) == goal, 1.0, 0.0).astype(jnp.bfloat16)
        sums[pl.ds(pl.multiple_of(first, block), block), :] = jnp.dot(
            hot, got[...].reshape(-1, LANES), preferred_element_type=jnp.float32
        ).astype(jnp.bfloat16)
        for o in range(0 if k else 1, pair_count):
            other = row * pair_count + lax.rem(my_pair + o, pair_count)
            sum_copy(other, me).start()
    parts[me] = sums[pl.ds(pl.multiple_of(me * tiles, tiles), tiles), :]
    for o in offsets:
        other = lax.rem(me + o, devices)
        sum_copy(other, other).wait_recv()

    low = iota((tiles, LANES), 1) < BLK
    half = devices * BLK
    for m in range(devices // 2):
        one, two = parts[2 * m].astype(jnp.float32), parts[2 * m + 1].astype(jnp.float32)
        to = m * LANES
        out_ref[:, to : to + LANES] = jnp.where(low, one, pltpu.roll(two, BLK, 1))
        out_ref[:, half + to : half + to + LANES] = jnp.where(low, pltpu.roll(one, BLK, 1), two)
    halo_up.wait_send()
    halo_down.wait_send()
    for o in offsets:
        other = lax.rem(me + o, devices)
        term_copy(other, me).wait_send()
        goal_copy(other, me).wait_send()
        sum_copy(other, me).wait_send()


def exchanged(a_tiles, p_tiles, a_cols, tile_group, targets, tiles):
    fine_rows = a_tiles.shape[0]
    count, q = fine_rows * KS, BLK // 2
    rows_count, pair_count = lax.axis_size("rows"), lax.axis_size("pair")
    devices = rows_count * pair_count
    code, group = row_codes(a_cols, tile_group)
    whole = pl.BlockSpec(memory_space=pltpu.VMEM)
    return pl.pallas_call(
        functools.partial(exchange_kernel, rows_count, pair_count),
        in_specs=[pl.BlockSpec(memory_space=pl.ANY)] + [whole] * 4,
        out_specs=whole,
        out_shape=jax.ShapeDtypeStruct((tiles, devices * LANES), jnp.float32),
        scratch_shapes=[
            pltpu.VMEM(a_tiles.shape, jnp.bfloat16),
            pltpu.VMEM(((fine_rows + 2 * HB) * LANES, LANES), jnp.bfloat16),
            pltpu.VMEM((q * KS * CHUNK, LANES), jnp.float32),
            pltpu.VMEM((2 * HB, q, LANES), jnp.bfloat16),
            pltpu.VMEM((devices, count, LANES), jnp.bfloat16),
            pltpu.VMEM((devices, count, LANES), jnp.bfloat16),
            pltpu.VMEM((devices, 1, count), jnp.int32),
            pltpu.VMEM((devices * tiles, LANES), jnp.bfloat16),
            pltpu.VMEM((devices, tiles, LANES), jnp.bfloat16),
            pltpu.SemaphoreType.DMA((4,)),
            pltpu.SemaphoreType.DMA((2,)),
            pltpu.SemaphoreType.DMA((2,)),
        ]
        + [pltpu.SemaphoreType.DMA((devices,))] * 6,
        compiler_params=pltpu.CompilerParams(
            collective_id=0, has_side_effects=True, vmem_limit_bytes=48 * 1024 * 1024
        ),
    )(a_tiles, p_tiles.reshape(fine_rows, q, LANES), code, group, targets)


def routed(terms, coarse_slots, aggregate):
    fine_rows = aggregate.shape[0]
    q = BLK // 2
    width = BLK * BLK
    rows_count, pair_count = lax.axis_size("rows"), lax.axis_size("pair")
    flat = terms.reshape(q, fine_rows // CHUNK, KS, CHUNK, 2, BLK)
    flat = flat.transpose(1, 3, 2, 4, 0, 5).reshape(fine_rows, KS, width)
    group_size = fine_rows // RATIO * pair_count
    capacity = 2 * fine_rows // rows_count
    dest_group = aggregate // group_size
    local_rows = aggregate - dest_group * group_size
    targets = local_rows[:, None] * KC + coarse_slots
    order = jnp.arange(fine_rows)
    same = (dest_group[:, None] == dest_group[None, :]) & (order[None, :] < order[:, None])
    position = dest_group * capacity + jnp.sum(same.astype(jnp.int32), axis=1)

    def exchange(values):
        buffer = jnp.zeros((rows_count * capacity,) + values.shape[1:], values.dtype)
        buffer = buffer.at[position].set(values)
        return lax.all_to_all(buffer, "rows", split_axis=0, concat_axis=0, tiled=True)

    got = exchange(flat).reshape(-1, width).astype(jnp.float32)
    panel = jax.ops.segment_sum(
        got, exchange(targets).reshape(-1), num_segments=group_size * KC
    )
    panel = panel.reshape(group_size, KC, width)
    return lax.psum_scatter(panel, "pair", scatter_dimension=0, tiled=True)


def body(a_tiles, p_tiles, a_cols, tile_group, coarse_slots, aggregate):
    fine_rows, width = p_tiles.shape
    devices = lax.axis_size(BOTH)
    if devices * LANES != width:
        return routed(local_terms(a_tiles, p_tiles, a_cols, tile_group), coarse_slots, aggregate)
    targets = in_term_order(aggregate[:, None] * KC + coarse_slots).reshape(1, -1)
    tiles = fine_rows // RATIO * KC
    result = exchanged(a_tiles, p_tiles, a_cols, tile_group, targets, tiles)
    return result.reshape(fine_rows // RATIO, KC, width)


def solution(mesh):
    return jax.shard_map(
        body,
        mesh=mesh,
        in_specs=(
            P(BOTH, None, None),
            P(BOTH, None),
            P(BOTH, None),
            P(BOTH, None),
            P(BOTH, None),
            P(BOTH),
        ),
        out_specs=P(BOTH, None, None),
        check_vma=False,
    )
```

```python
import functools

import jax
import jax.numpy as jnp
from jax import lax
from jax.experimental import pallas as pl
from jax.experimental.pallas import tpu as pltpu
from jax.sharding import PartitionSpec as P

BLK = 64
KA = 8
KS = 2
KC = 16
HB = 2
RATIO = 16
LANES = 128
NEAR = 2 * HB + 1
CHUNK = 8
STEPS = 8
BOTH = ("rows", "pair")


def extended(array, width):
    devices, length = lax.axis_size(BOTH), array.shape[0]
    up = [(i, i + 1) for i in range(devices - 1)]
    down = [(j, i) for i, j in up]
    before = lax.ppermute(array[length - width :], BOTH, up)
    after = lax.ppermute(array[:width], BOTH, down)
    return jnp.concatenate([before, array, after], axis=0)


def iota(shape, dim):
    return lax.broadcasted_iota(jnp.int32, shape, dim)


def put_diagonal(flat, want, low):
    flat = flat.astype(jnp.float32)
    turned = pltpu.roll(flat, BLK, 1)
    zero = jnp.zeros_like(flat)
    parts = jnp.concatenate(
        [
            jnp.where(low, flat, zero),
            jnp.where(low, turned, zero),
            jnp.where(low, zero, turned),
            jnp.where(low, zero, flat),
        ],
        axis=0,
    ).astype(jnp.bfloat16)
    return jnp.dot(want, parts, preferred_element_type=jnp.float32).astype(jnp.bfloat16)


def constants():
    q = BLK // 2
    r, k = iota((LANES, LANES), 0), iota((LANES, LANES), 1)
    want = jnp.where(
        (r // BLK == k // BLK) & (r % BLK == 2 * (k % q) + (k // q) % 2), 1.0, 0.0
    ).astype(jnp.bfloat16)
    eye = jnp.where(r == k, 1.0, 0.0).astype(jnp.bfloat16)
    spread = jnp.where(
        iota((q, q * KA), 0) == iota((q, q * KA), 1) // KA, 1.0, 0.0
    ).astype(jnp.bfloat16)
    low = iota((q, LANES), 1) < BLK
    return want, eye, spread, low


def row_terms(read, code, group, near, own, eye, spread, low):
    q = BLK // 2
    tiles = jnp.concatenate([read(c).astype(jnp.float32) for c in range(q)], axis=0)
    tiles = tiles.astype(jnp.bfloat16)

    def picked(j):
        one = jnp.where(code == j, 1.0, 0.0)
        pair = jnp.concatenate([one, one], axis=0).astype(jnp.bfloat16)
        return jnp.broadcast_to(pair[None], (q // 2,) + pair.shape).reshape(tiles.shape)

    left = jnp.concatenate([tiles * picked(j) for j in range(NEAR)], axis=1)
    products = jnp.dot(left, near, preferred_element_type=jnp.float32).astype(jnp.bfloat16)
    turned = lax.dot_general(
        eye, own, (((1,), (1,)), ((), ())), preferred_element_type=jnp.float32
    ).astype(jnp.bfloat16)
    wide = jnp.dot(turned, spread, preferred_element_type=jnp.float32).astype(jnp.bfloat16)
    rows = jnp.concatenate(
        [wide * jnp.where(group == s, 1.0, 0.0).astype(jnp.bfloat16) for s in range(KS)], axis=0
    )
    full = jnp.dot(rows, products, preferred_element_type=jnp.float32)
    terms = []
    for s in range(KS):
        part = full[s * LANES : (s + 1) * LANES]
        terms.append(
            jnp.where(low, part[:q], part[3 * q :])
            + pltpu.roll(jnp.where(low, part[q : 2 * q], part[2 * q : 3 * q]), BLK, 1)
        )
    return terms


def terms_kernel(a_ref, p_ref, code_ref, group_ref, out_ref, diag, stage):
    step = pl.program_id(0)
    q = BLK // 2
    want, eye, spread, low = constants()

    @pl.when(step == 0)
    def _():
        def one(t, _):
            diag[pl.ds(pl.multiple_of(t * LANES, LANES), LANES), :] = put_diagonal(p_ref[t], want, low)
            return 0

        lax.fori_loop(0, p_ref.shape[0], one, 0, unroll=4)

    for i in range(CHUNK):
        row = step * CHUNK + i
        terms = row_terms(
            lambda c: a_ref[i, :, c * LANES : (c + 1) * LANES],
            code_ref[i],
            group_ref[i],
            diag[pl.ds(pl.multiple_of(row * LANES, LANES), NEAR * LANES), :],
            p_ref[row + HB],
            eye,
            spread,
            low,
        )
        for s in range(KS):
            stage[pl.ds(s * CHUNK + i, q, stride=KS * CHUNK), :] = terms[s]
    out_ref[...] = stage[...].astype(jnp.bfloat16).reshape(out_ref.shape)


def row_codes(a_cols, tile_group):
    fine_rows = a_cols.shape[0]
    q = BLK // 2
    own = lax.axis_index(BOTH) * fine_rows + jnp.arange(fine_rows, dtype=jnp.int32)
    offset = a_cols - own[:, None] + HB
    code = jnp.broadcast_to(offset[:, :, None], (fine_rows, KA, LANES))
    group = jnp.tile(tile_group, (1, q)).reshape(fine_rows, 1, q * KA)
    return code, group


def local_terms(a_tiles, p_tiles, a_cols, tile_group):
    fine_rows = a_tiles.shape[0]
    q = BLK // 2
    near_p = extended(p_tiles, HB).reshape(fine_rows + 2 * HB, q, LANES)
    code, group = row_codes(a_cols, tile_group)
    steps = fine_rows // CHUNK
    return pl.pallas_call(
        terms_kernel,
        grid=(steps,),
        in_specs=[
            pl.BlockSpec((CHUNK, KA, BLK * BLK), lambda g: (g, 0, 0)),
            pl.BlockSpec((fine_rows + 2 * HB, q, LANES), lambda g: (0, 0, 0)),
            pl.BlockSpec((CHUNK, KA, LANES), lambda g: (g, 0, 0)),
            pl.BlockSpec((CHUNK, 1, q * KA), lambda g: (g, 0, 0)),
        ],
        out_specs=pl.BlockSpec((q, KS * CHUNK, LANES), lambda g: (0, g, 0)),
        out_shape=jax.ShapeDtypeStruct((q, fine_rows * KS, LANES), jnp.bfloat16),
        scratch_shapes=[
            pltpu.VMEM(((fine_rows + 2 * HB) * LANES, LANES), jnp.bfloat16),
            pltpu.VMEM((q * KS * CHUNK, LANES), jnp.float32),
        ],
        compiler_params=pltpu.CompilerParams(vmem_limit_bytes=40 * 1024 * 1024),
    )(a_tiles, near_p, code, group)


def in_term_order(values):
    rows = values.shape[0]
    return values.reshape(rows // CHUNK, CHUNK, KS).transpose(0, 2, 1).reshape(rows * KS)


def exchange_kernel(rows_count, pair_count, a_hbm, p_ref, code_ref, group_ref, target_ref, out_ref, a_ref, diag, stage, halo, term_ref, got, goals, sums, parts, a_came, halo_sent, halo_came, sent, came, goal_sent, goal_came, sum_sent, sum_came):
    my_row, my_pair = lax.axis_index("rows"), lax.axis_index("pair")
    devices = rows_count * pair_count
    me = my_row * pair_count + my_pair
    tiles = parts.shape[1]
    block = pair_count * tiles

    def at(device):
        return (lax.div(device, pair_count), lax.rem(device, pair_count))

    def copy(src, dst, send_sem, recv_sem, device):
        return pltpu.make_async_remote_copy(
            src_ref=src,
            dst_ref=dst,
            send_sem=send_sem,
            recv_sem=recv_sem,
            device_id=at(device),
            device_id_type=pl.DeviceIdType.MESH,
        )

    fine_rows = p_ref.shape[0]
    q = BLK // 2
    steps = STEPS
    span = fine_rows // steps
    terms_span = span * KS
    ahead, behind = lax.rem(me + 1, devices), lax.rem(me + devices - 1, devices)

    def a_copy(step):
        rows = pl.ds(pl.multiple_of(lax.rem(step + 1, steps) * span, span), span)
        return pltpu.make_async_copy(a_hbm.at[rows], a_ref.at[rows], a_came.at[step])

    def term_copy(device, slot):
        return copy(term_ref.at[device], got.at[slot], sent.at[device], came.at[slot], device)

    def term_part(device, slot, part):
        rows = pl.ds(pl.multiple_of(part * terms_span, terms_span), terms_span)
        return copy(term_ref.at[device, rows], got.at[slot, rows], sent.at[device], came.at[slot], device)

    halo_up = copy(p_ref.at[pl.ds(fine_rows - HB, HB)], halo.at[pl.ds(0, HB)], halo_sent.at[0], halo_came.at[0], ahead)
    halo_down = copy(p_ref.at[pl.ds(0, HB)], halo.at[pl.ds(HB, HB)], halo_sent.at[1], halo_came.at[1], behind)

    def goal_copy(device, slot):
        return copy(target_ref, goals.at[slot], goal_sent.at[device], goal_came.at[slot], device)

    def sum_copy(device, slot):
        rows = pl.ds(pl.multiple_of(device * tiles, tiles), tiles)
        return copy(sums.at[rows], parts.at[slot], sum_sent.at[device], sum_came.at[slot], device)

    barrier = pltpu.get_barrier_semaphore()
    offsets = sorted(range(1, devices), key=lambda o: abs(o - devices // 2))
    for o in offsets:
        pl.semaphore_signal(
            barrier, inc=1, device_id=at(lax.rem(me + o, devices)), device_id_type=pl.DeviceIdType.MESH
        )
    for step in range(steps):
        a_copy(step).start()
    want, eye, spread, low = constants()

    def own_diagonal(t, _):
        diag[pl.ds(pl.multiple_of((t + HB) * LANES, LANES), LANES), :] = put_diagonal(p_ref[t], want, low)
        return 0

    lax.fori_loop(0, fine_rows, own_diagonal, 0, unroll=4)
    pl.semaphore_wait(barrier, devices - 1)
    halo_up.start()
    halo_down.start()
    for o in offsets:
        other = lax.rem(me + o, devices)
        goal_copy(other, me).start()
    goals[me] = target_ref[...]

    def quarter(step, _):
        part = lax.rem(step + 1, steps)
        a_copy(step).wait()

        @pl.when(step == steps - 2)
        def _():
            halo_up.wait_recv()
            halo_down.wait_recv()
            for t in range(HB):
                diag[t * LANES : (t + 1) * LANES, :] = put_diagonal(halo[t], want, low)
                last = fine_rows + HB + t
                diag[last * LANES : (last + 1) * LANES, :] = put_diagonal(halo[HB + t], want, low)

        def chunk(c, _):
            at_chunk = part * (span // CHUNK) + c

            for i in range(CHUNK):
                row = at_chunk * CHUNK + i
                terms = row_terms(
                    lambda col: a_ref[row, :, col * LANES : (col + 1) * LANES],
                    code_ref[row],
                    group_ref[row],
                    diag[pl.ds(pl.multiple_of(row * LANES, LANES), NEAR * LANES), :],
                    p_ref[row],
                    eye,
                    spread,
                    low,
                )
                for s in range(KS):
                    stage[pl.ds(s * CHUNK + i, q, stride=KS * CHUNK), :] = terms[s]
            rows = pl.ds(pl.multiple_of(at_chunk * KS * CHUNK, KS * CHUNK), KS * CHUNK)
            term_ref[:, rows, :] = stage[...].astype(jnp.bfloat16).reshape(q, KS * CHUNK, LANES)
            return 0

        lax.fori_loop(0, span // CHUNK, chunk, 0)
        for o in offsets:
            term_part(lax.rem(me + o, devices), me, part).start()
        return 0

    lax.fori_loop(0, steps, quarter, 0)
    got[me] = term_ref[me]
    for o in offsets[::-1]:
        other = lax.rem(me + o, devices)
        goal_copy(other, other).wait_recv()
        term_copy(other, other).wait_recv()

    goal = jnp.concatenate([goals[j] for j in range(devices)], axis=1)
    for k in sorted(range(rows_count), key=lambda o: abs(o - rows_count // 2)):
        row = lax.rem(my_row + k, rows_count)
        first = row * block
        hot = jnp.where(first + iota((block, goal.shape[1]), 0) == goal, 1.0, 0.0).astype(jnp.bfloat16)
        sums[pl.ds(pl.multiple_of(first, block), block), :] = jnp.dot(
            hot, got[...].reshape(-1, LANES), preferred_element_type=jnp.float32
        ).astype(jnp.bfloat16)
        for o in range(0 if k else 1, pair_count):
            other = row * pair_count + lax.rem(my_pair + o, pair_count)
            sum_copy(other, me).start()
    parts[me] = sums[pl.ds(pl.multiple_of(me * tiles, tiles), tiles), :]
    for o in offsets:
        other = lax.rem(me + o, devices)
        sum_copy(other, other).wait_recv()

    low = iota((tiles, LANES), 1) < BLK
    half = devices * BLK
    for m in range(devices // 2):
        one, two = parts[2 * m].astype(jnp.float32), parts[2 * m + 1].astype(jnp.float32)
        to = m * LANES
        out_ref[:, to : to + LANES] = jnp.where(low, one, pltpu.roll(two, BLK, 1))
        out_ref[:, half + to : half + to + LANES] = jnp.where(low, pltpu.roll(one, BLK, 1), two)
    halo_up.wait_send()
    halo_down.wait_send()
    for o in offsets:
        other = lax.rem(me + o, devices)
        term_copy(other, me).wait_send()
        goal_copy(other, me).wait_send()
        sum_copy(other, me).wait_send()


def exchanged(a_tiles, p_tiles, a_cols, tile_group, targets, tiles):
    fine_rows = a_tiles.shape[0]
    count, q = fine_rows * KS, BLK // 2
    rows_count, pair_count = lax.axis_size("rows"), lax.axis_size("pair")
    devices = rows_count * pair_count
    code, group = row_codes(a_cols, tile_group)
    whole = pl.BlockSpec(memory_space=pltpu.VMEM)
    return pl.pallas_call(
        functools.partial(exchange_kernel, rows_count, pair_count),
        in_specs=[pl.BlockSpec(memory_space=pltpu.HBM)] + [whole] * 4,
        out_specs=whole,
        out_shape=jax.ShapeDtypeStruct((tiles, devices * LANES), jnp.float32),
        scratch_shapes=[
            pltpu.VMEM(a_tiles.shape, jnp.bfloat16),
            pltpu.VMEM(((fine_rows + 2 * HB) * LANES, LANES), jnp.bfloat16),
            pltpu.VMEM((q * KS * CHUNK, LANES), jnp.float32),
            pltpu.VMEM((2 * HB, q, LANES), jnp.bfloat16),
            pltpu.VMEM((devices, count, LANES), jnp.bfloat16),
            pltpu.VMEM((devices, count, LANES), jnp.bfloat16),
            pltpu.VMEM((devices, 1, count), jnp.int32),
            pltpu.VMEM((devices * tiles, LANES), jnp.bfloat16),
            pltpu.VMEM((devices, tiles, LANES), jnp.bfloat16),
            pltpu.SemaphoreType.DMA((STEPS,)),
            pltpu.SemaphoreType.DMA((2,)),
            pltpu.SemaphoreType.DMA((2,)),
        ]
        + [pltpu.SemaphoreType.DMA((devices,))] * 6,
        compiler_params=pltpu.CompilerParams(
            collective_id=0, has_side_effects=True, vmem_limit_bytes=48 * 1024 * 1024
        ),
    )(a_tiles, p_tiles.reshape(fine_rows, q, LANES), code, group, targets)


def routed(terms, coarse_slots, aggregate):
    fine_rows = aggregate.shape[0]
    q = BLK // 2
    width = BLK * BLK
    rows_count, pair_count = lax.axis_size("rows"), lax.axis_size("pair")
    flat = terms.reshape(q, fine_rows // CHUNK, KS, CHUNK, 2, BLK)
    flat = flat.transpose(1, 3, 2, 4, 0, 5).reshape(fine_rows, KS, width)
    group_size = fine_rows // RATIO * pair_count
    capacity = 2 * fine_rows // rows_count
    dest_group = aggregate // group_size
    local_rows = aggregate - dest_group * group_size
    targets = local_rows[:, None] * KC + coarse_slots
    order = jnp.arange(fine_rows)
    same = (dest_group[:, None] == dest_group[None, :]) & (order[None, :] < order[:, None])
    position = dest_group * capacity + jnp.sum(same.astype(jnp.int32), axis=1)

    def exchange(values):
        buffer = jnp.zeros((rows_count * capacity,) + values.shape[1:], values.dtype)
        buffer = buffer.at[position].set(values)
        return lax.all_to_all(buffer, "rows", split_axis=0, concat_axis=0, tiled=True)

    got = exchange(flat).reshape(-1, width).astype(jnp.float32)
    panel = jax.ops.segment_sum(
        got, exchange(targets).reshape(-1), num_segments=group_size * KC
    )
    panel = panel.reshape(group_size, KC, width)
    return lax.psum_scatter(panel, "pair", scatter_dimension=0, tiled=True)


def body(a_tiles, p_tiles, a_cols, tile_group, coarse_slots, aggregate):
    fine_rows, width = p_tiles.shape
    devices = lax.axis_size(BOTH)
    if devices * LANES != width:
        return routed(local_terms(a_tiles, p_tiles, a_cols, tile_group), coarse_slots, aggregate)
    targets = in_term_order(aggregate[:, None] * KC + coarse_slots).reshape(1, -1)
    tiles = fine_rows // RATIO * KC
    result = exchanged(a_tiles, p_tiles, a_cols, tile_group, targets, tiles)
    return result.reshape(fine_rows // RATIO, KC, width)


def solution(mesh):
    return jax.shard_map(
        body,
        mesh=mesh,
        in_specs=(
            P(BOTH, None, None),
            P(BOTH, None),
            P(BOTH, None),
            P(BOTH, None),
            P(BOTH, None),
            P(BOTH),
        ),
        out_specs=P(BOTH, None, None),
        check_vma=False,
    )
```
